1024 devices in a mesh: dp: 128 (over z_lo, y, core), tensor: 8 (over z_hi, x).
Axes of the slice: x: 4, y: 8, z: 16 (z_hi: 2, z_lo: 8; z = z_hi * 8 + z_lo), core: 2. Of those that a mesh axis runs over, the one named last changes fastest.
Arguments:
- image_features: bfloat16 [8192, 1152], P('dp', 'tensor'), may hold values from -40 to 40
- text_features: bfloat16 [8192, 1152], P('dp', 'tensor'), may hold values from -40 to 40
- image_weight: bfloat16 [1152, 1152], P('tensor'), may hold values from -0.1875 to 0.1875
- text_weight: bfloat16 [1152, 1152], P('tensor'), may hold values from -0.1875 to 0.1875
- log_scale: float32 [1], replicated, may hold values from 1.5 to 2.5
- logit_bias: float32 [1], replicated, may hold values from -4 to -2
Outputs:
- image_weight_grad: float32 [1152, 1152], P('tensor', 'dp')
- text_weight_grad: float32 [1152, 1152], P('tensor', 'dp')
- image_feature_grad: float32 [8192, 1152], P('dp', 'tensor')
- text_feature_grad: float32 [8192, 1152], P('dp', 'tensor')
The draws below stay inside these ranges and needn't reach their ends.
All inputs are finite; a program needn't handle non-finite values.
Results may differ from the reference program's by a relative error of at most 0.005.
Values may be sent and summed in bfloat16 or wider, within the bound.
No kernel may reach another device: no remote copies, remote signals or barrier semaphores. Data moves between devices by JAX's collectives and lax.ppermute only.
A program may use at most 32 MiB of HBM per device.

```python
import math
import jax
import jax.numpy as jnp
from jax import lax

D = 1152
E = 1152
PAIRS = 8192


def draw_image_features(key, part):
    key = jax.random.fold_in(key, 11)
    first, second = jax.random.split(key, 2)
    scales = jnp.exp(jax.random.uniform(second, (PAIRS, 1), jnp.float32, 0.0, math.log(10.0)))
    base = jnp.clip(jax.random.normal(first, (PAIRS, D), jnp.float32), -4.0, 4.0)
    return (base * scales).astype(jnp.bfloat16)


def draw_text_features(key, part):
    key = jax.random.fold_in(key, 23)
    first, second = jax.random.split(key, 2)
    scales = jnp.exp(jax.random.uniform(second, (PAIRS, 1), jnp.float32, 0.0, math.log(10.0)))
    base = jnp.clip(jax.random.normal(first, (PAIRS, D), jnp.float32), -4.0, 4.0)
    return (base * scales).astype(jnp.bfloat16)


def block_levels(own_key, dims, cuts, smallest, largest):
    gain, own = 1.0, jax.random.fold_in(own_key, 6)
    for position, parts in cuts:
        steps = jnp.exp(jax.random.uniform(jax.random.fold_in(own, position), (parts,), jnp.float32, smallest / len(cuts), largest / len(cuts)))
        gain = gain * jnp.repeat(steps, dims[position] // parts).reshape([-1 if axis == position else 1 for axis in range(len(dims))])
    return gain


def normal_values(own_key, extent, width, reach, pieces=(), kind=jnp.bfloat16):
    loudness = block_levels(own_key, extent, pieces, -0.22, 0.18) if pieces else 1.0
    result = jax.random.normal(own_key, extent, jnp.float32) * width * loudness
    return jnp.minimum(jnp.maximum(result, -reach), reach).astype(kind)


def setup_inputs(seed: int = 0) -> dict:
    key_of = jax.random.split(jax.random.key(seed), 7)
    image_features = draw_image_features(jax.random.fold_in(key_of[6], 71), 0)
    text_features = draw_text_features(jax.random.fold_in(key_of[6], 71), 0)
    image_weight = normal_values(key_of[2], (D, E), D ** -0.5, 0.1875, ((0, 8),))
    text_weight = normal_values(key_of[3], (D, E), D ** -0.5, 0.1875, ((0, 8),))
    log_scale = jnp.clip(jax.random.uniform(key_of[4], (1,), jnp.float32, 1.5, 2.5), 1.5, 2.5)
    logit_bias = jnp.clip(jax.random.uniform(key_of[5], (1,), jnp.float32, -4.0, -2.0), -4.0, -2.0)
    return dict(image_features=image_features, text_features=text_features, image_weight=image_weight, text_weight=text_weight, log_scale=log_scale, logit_bias=logit_bias)


EPS = 1e-06

def normalize(embed):
    inverse = lax.rsqrt(lax.optimization_barrier(jnp.sum(embed * embed, axis=-1, keepdims=True)) + EPS)
    return (embed * inverse, inverse)

def direction_sum(own_vec, other_vec, scale, bias):
    block = math.gcd(PAIRS, 512)
    count = PAIRS // block
    blocks = own_vec.reshape(count, block, own_vec.shape[1])
    starts = jnp.arange(count, dtype=jnp.int32) * block

    def one_block(item):
        rows_vec, start = item
        logits = scale * jnp.dot(rows_vec, other_vec.T, preferred_element_type=jnp.float32) + bias
        rows = lax.broadcasted_iota(jnp.int32, logits.shape, 0) + start
        cols = lax.broadcasted_iota(jnp.int32, logits.shape, 1)
        target = jnp.where(rows == cols, 1.0, 0.0).astype(jnp.float32)
        coef = (jax.nn.sigmoid(logits) - target).astype(jnp.bfloat16)
        return jnp.dot(coef, other_vec, preferred_element_type=jnp.float32)
    return lax.map(one_block, (blocks, starts)).reshape(PAIRS, other_vec.shape[1])

def back_norm(direction, unit, inverse):
    inner = lax.optimization_barrier(jnp.sum(unit * direction, axis=-1, keepdims=True))
    return (inverse * (direction - unit * inner)).astype(jnp.bfloat16)

def reference(image_features, text_features, image_weight, text_weight, log_scale, logit_bias):
    scale = jnp.exp(log_scale[0])
    bias = logit_bias[0]
    image_embed = jnp.dot(image_features, image_weight, preferred_element_type=jnp.float32)
    text_embed = jnp.dot(text_features, text_weight, preferred_element_type=jnp.float32)
    image_unit, image_inverse = normalize(image_embed)
    text_unit, text_inverse = normalize(text_embed)
    image_vec = image_unit.astype(jnp.bfloat16)
    text_vec = text_unit.astype(jnp.bfloat16)
    image_dir = scale * direction_sum(image_vec, text_vec, scale, bias)
    text_dir = scale * direction_sum(text_vec, image_vec, scale, bias)
    image_back = back_norm(image_dir, image_unit, image_inverse)
    text_back = back_norm(text_dir, text_unit, text_inverse)
    image_weight_grad = jnp.dot(image_features.T, image_back, preferred_element_type=jnp.float32)
    text_weight_grad = jnp.dot(text_features.T, text_back, preferred_element_type=jnp.float32)
    image_feature_grad = jnp.dot(image_back, image_weight.T, preferred_element_type=jnp.float32)
    text_feature_grad = jnp.dot(text_back, text_weight.T, preferred_element_type=jnp.float32)
    return (image_weight_grad, text_weight_grad, image_feature_grad, text_feature_grad)
```

```python
import jax
import jax.numpy as jnp
from jax import lax
from jax.sharding import Mesh, PartitionSpec as P

EPS = 1e-06
DATA = ("zl", "y", "c")
TENSOR = ("zh", "x")
SIZES = {"zl": 8, "y": 8, "c": 2, "zh": 2, "x": 4}
F32 = jnp.float32
BF16 = jnp.bfloat16


def dot(a, b, dims):
    return lax.dot_general(a, b, (dims, ((), ())), preferred_element_type=F32)


def exchange(blocks, axes):
    return lax.all_to_all(blocks, axes, 0, 0, tiled=True)


def spread(block, axes, count):
    return exchange(jnp.broadcast_to(block[None], (count, *block.shape)), axes)


def shifted(value, axis, by):
    size = SIZES[axis]
    return lax.ppermute(value, axis, [(i, (i + by) % size) for i in range(size)])


def flat(*sizes):
    return [lax.broadcasted_iota(jnp.int32, sizes, i).reshape(-1) for i in range(len(sizes))]


def local(image_features, text_features, image_weight, text_weight, log_scale, logit_bias):
    scale = jnp.exp(log_scale[0])
    bias = logit_bias[0]
    zl, y, c, zh, x = (lax.axis_index(axis) for axis in ("zl", "y", "c", "zh", "x"))
    rows, depth = image_features.shape
    width = image_weight.shape[1]
    tensor = SIZES["zh"] * SIZES["x"]
    own = rows // tensor
    both = 2 * own

    with jax.named_scope("embed"):
        parts = [
            dot(features, weight, ((1,), (0,))).astype(BF16).reshape(tensor, own, width)
            for features, weight in ((image_features, image_weight), (text_features, text_weight))
        ]
        parts = exchange(jnp.concatenate(parts, axis=1), TENSOR)
        embed = jnp.sum(parts.astype(F32), axis=0)
        inverse = lax.rsqrt(jnp.sum(embed * embed, axis=-1, keepdims=True) + EPS)
        unit = embed * inverse
        vec = unit.astype(BF16)

    with jax.named_scope("gather_own"):
        mine = spread(vec, "y", SIZES["y"]).reshape(-1, width)
        theirs = shifted(mine, "c", 1)
        held = jnp.concatenate([mine, theirs])

    with jax.named_scope("gather_others"):
        column = lax.all_gather(vec, ("zh", "zl"), tiled=True)
        steps = (0, 1, 3, 2)
        others = jnp.concatenate([column] + [shifted(column, "x", by) for by in steps[1:]])

    with jax.named_scope("pairs"):
        hc, hy, hkind, hrow = flat(2, SIZES["y"], 2, own)
        held_data = (zl * SIZES["y"] + hy) * 2 + jnp.where(hc == 0, c, 1 - c)
        held_id = held_data * rows + (zh * SIZES["x"] + x) * own + hrow
        ox, ozh, ozl, okind, orow = flat(4, 2, SIZES["zl"], 2, own)
        step = jnp.where(ox == 0, 0, jnp.where(ox == 1, 1, jnp.where(ox == 2, 3, 2)))
        other_data = (ozl * SIZES["y"] + y) * 2 + c
        other_id = other_data * rows + (ozh * SIZES["x"] + (x - step + 4) % 4) * own + orow
        logits = scale * dot(held, others, ((1,), (1,))) + bias
        target = jnp.where(held_id[:, None] == other_id[None, :], 1.0, 0.0)
        coef = jnp.where(hkind[:, None] != okind[None, :], jax.nn.sigmoid(logits) - target, 0.0)
        direction = dot(coef.astype(BF16), others, ((1,), (0,)))

    with jax.named_scope("reduce_pairs"):
        half = mine.shape[0]
        direction = direction[:half] + shifted(direction[half:], "c", 1)
        direction = exchange(direction.astype(BF16).reshape(SIZES["y"], both, width), "y")
        direction = scale * jnp.sum(direction.astype(F32), axis=0)

    with jax.named_scope("back"):
        inner = jnp.sum(unit * direction, axis=-1, keepdims=True)
        back = (inverse * (direction - unit * inner)).astype(BF16)
        back = spread(back, TENSOR, tensor).reshape(-1, width)

    with jax.named_scope("feature_grad"):
        weights = jnp.concatenate([image_weight, text_weight])
        grads = dot(back, weights, ((1,), (1,))).reshape(tensor, 2, own, 2 * depth)
        image_feature_grad = grads[:, 0, :, :depth].reshape(rows, depth)
        text_feature_grad = grads[:, 1, :, depth:].reshape(rows, depth)

    with jax.named_scope("weight_grad"):
        blank = jnp.zeros((tensor, own, depth), BF16)
        features = jnp.concatenate(
            [
                jnp.concatenate([image_features.reshape(tensor, own, depth), blank], axis=2),
                jnp.concatenate([blank, text_features.reshape(tensor, own, depth)], axis=2),
            ],
            axis=1,
        ).reshape(2 * rows, 2 * depth)
        share = width // (SIZES["zl"] * SIZES["y"] * 2)
        pc, py, pzl, pk = flat(2, SIZES["y"], SIZES["zl"], share)
        source = ((pzl * SIZES["y"] + py) * 2 + jnp.where(pc == 0, c, 1 - c)) * share + pk
        order = lax.broadcasted_iota(jnp.int32, (width, width), 0) == source[None, :]
        sorted_back = dot(back, order.astype(BF16), ((1,), (0,))).astype(BF16)
        partial = dot(sorted_back, features, ((0,), (0,)))
        partial = partial[: width // 2] + shifted(partial[width // 2 :], "c", 1)
        partial = exchange(partial.astype(BF16).reshape(SIZES["y"], -1, 2 * depth), "y")
        partial = jnp.sum(partial.astype(F32), axis=0)
        partial = exchange(partial.reshape(SIZES["zl"], share, 2 * depth), "zl")
        total = jnp.sum(partial, axis=0).T

    return (total[:depth], total[depth:], image_feature_grad, text_feature_grad)


def solution(mesh):
    names = ("zl", "y", "c", "zh", "x")
    fine = Mesh(mesh.devices.reshape([SIZES[name] for name in names]), names)
    placed = (P(DATA, TENSOR), P(DATA, TENSOR), P(TENSOR, None), P(TENSOR, None), P(), P())
    return jax.shard_map(
        local,
        mesh=fine,
        in_specs=placed,
        out_specs=(P(TENSOR, DATA), P(TENSOR, DATA), P(DATA, TENSOR), P(DATA, TENSOR)),
        check_vma=False,
    )
```

```python
import jax
import jax.numpy as jnp
from jax import lax
from jax.sharding import Mesh, PartitionSpec as P

EPS = 1e-06
DATA = ("zl", "y", "c")
TENSOR = ("zh", "x")
SIZES = {"zl": 8, "y": 8, "c": 2, "zh": 2, "x": 4}
F32 = jnp.float32
BF16 = jnp.bfloat16


def dot(a, b, dims):
    return lax.dot_general(a, b, (dims, ((), ())), preferred_element_type=F32)


def exchange(blocks, axes):
    return lax.all_to_all(blocks, axes, 0, 0, tiled=True)


def spread(block, axes, count):
    return exchange(jnp.broadcast_to(block[None], (count, *block.shape)), axes)


def shifted(value, axis, by):
    size = SIZES[axis]
    return lax.ppermute(value, axis, [(i, (i + by) % size) for i in range(size)])


def flat(*sizes):
    return [lax.broadcasted_iota(jnp.int32, sizes, i).reshape(-1) for i in range(len(sizes))]


def local(image_features, text_features, image_weight, text_weight, log_scale, logit_bias):
    scale = jnp.exp(log_scale[0])
    bias = logit_bias[0]
    zl, y, c, zh, x = (lax.axis_index(axis) for axis in ("zl", "y", "c", "zh", "x"))
    rows, depth = image_features.shape
    width = image_weight.shape[1]
    own = rows // SIZES["x"]

    with jax.named_scope("embed"):
        parts = [
            dot(features, weight, ((1,), (0,))).astype(BF16).reshape(SIZES["x"], own, width)
            for features, weight in ((image_features, image_weight), (text_features, text_weight))
        ]
        parts = exchange(jnp.concatenate(parts, axis=1), "x")
        embed = jnp.sum(parts.astype(F32), axis=0)
        embed = embed + shifted(embed, "zh", 1)
        inverse = lax.rsqrt(jnp.sum(embed * embed, axis=-1, keepdims=True) + EPS)
        unit = embed * inverse
        vec = unit.astype(BF16)

    with jax.named_scope("gather_own"):
        mine = spread(vec, "y", SIZES["y"]).reshape(SIZES["y"], 2, own, width)
        mine = mine.transpose(1, 0, 2, 3).reshape(2, -1, width)
        theirs = shifted(mine, "c", 1)
        held = jnp.concatenate([mine, theirs], axis=1)

    with jax.named_scope("gather_others"):
        half = own // 2
        column = lax.dynamic_slice_in_dim(vec.reshape(2, own, width), zh * half, half, axis=1)
        column = lax.all_gather(column.reshape(2 * half, width), ("zh", "zl"), tiled=True)
        column = column.reshape(-1, 2, half, width).transpose(1, 0, 2, 3).reshape(2, -1, width)
        others = [column] + [shifted(column, "x", by) for by in (1, 3, 2)]

    with jax.named_scope("pairs"):
        hc, hy, hrow = flat(2, SIZES["y"], own)
        held_data = (zl * SIZES["y"] + hy) * 2 + jnp.where(hc == 0, c, 1 - c)
        held_id = held_data * rows + x * own + hrow
        ozh, ozl, orow = flat(2, SIZES["zl"], half)
        other_id = ((ozl * SIZES["y"] + y) * 2 + c) * rows + ozh * half + orow
        sums = [0.0, 0.0]
        for first, second in ((0, 1), (3, 2)):
            places = [(x + SIZES["x"] - by) % SIZES["x"] for by in (first, second)]
            ids = jnp.concatenate([other_id + place * own for place in places])
            pick = {0: 0, 1: 1, 3: 2, 2: 3}
            for kind in range(2):
                block = jnp.concatenate([others[pick[by]][1 - kind] for by in (first, second)])
                logits = scale * dot(held[kind], block, ((1,), (1,))) + bias
                target = jnp.where(held_id[:, None] == ids[None, :], 1.0, 0.0)
                coef = (jax.nn.sigmoid(logits) - target).astype(BF16)
                sums[kind] = sums[kind] + dot(coef, block, ((1,), (0,)))

    with jax.named_scope("reduce_pairs"):
        cut = SIZES["y"] * own
        sent = shifted(jnp.stack([total[cut:] for total in sums]), "c", 1)
        direction = jnp.stack([total[:cut] for total in sums]) + sent
        direction = direction.astype(BF16).reshape(2, SIZES["y"], own, width).transpose(1, 0, 2, 3)
        direction = exchange(direction.reshape(SIZES["y"], 2 * own, width), "y")
        direction = scale * jnp.sum(direction.astype(F32), axis=0)

    with jax.named_scope("back"):
        inner = jnp.sum(unit * direction, axis=-1, keepdims=True)
        back = (inverse * (direction - unit * inner)).astype(BF16)
        back = spread(back, "x", SIZES["x"]).reshape(-1, width)

    with jax.named_scope("feature_grad"):
        weights = jnp.concatenate([image_weight, text_weight])
        grads = dot(back, weights, ((1,), (1,))).reshape(SIZES["x"], 2, own, 2 * depth)
        image_feature_grad = grads[:, 0, :, :depth].reshape(rows, depth)
        text_feature_grad = grads[:, 1, :, depth:].reshape(rows, depth)

    with jax.named_scope("weight_grad"):
        blank = jnp.zeros((SIZES["x"], own, depth), BF16)
        features = jnp.concatenate(
            [
                jnp.concatenate([image_features.reshape(SIZES["x"], own, depth), blank], axis=2),
                jnp.concatenate([blank, text_features.reshape(SIZES["x"], own, depth)], axis=2),
            ],
            axis=1,
        ).reshape(2 * rows, 2 * depth)
        chips = SIZES["zl"] * SIZES["y"]
        share = width // (chips * 2)
        pc, pchip, pk = flat(2, chips, share)
        source = (pchip * 2 + jnp.where(pc == 0, c, 1 - c)) * share + pk
        order = lax.broadcasted_iota(jnp.int32, (width, width), 0) == source[None, :]
        sorted_back = dot(back, order.astype(BF16), ((1,), (0,))).astype(BF16)
        partial = dot(sorted_back, features, ((0,), (0,)))
        partial = partial[: width // 2] + shifted(partial[width // 2 :], "c", 1)
        partial = exchange(partial.astype(BF16).reshape(chips, share, 2 * depth), ("zl", "y"))
        total = jnp.sum(partial.astype(F32), axis=0).T

    return (total[:depth], total[depth:], image_feature_grad, text_feature_grad)


def solution(mesh):
    names = ("zl", "y", "c", "zh", "x")
    fine = Mesh(mesh.devices.reshape([SIZES[name] for name in names]), names)
    placed = (P(DATA, TENSOR), P(DATA, TENSOR), P(TENSOR, None), P(TENSOR, None), P(), P())
    return jax.shard_map(
        local,
        mesh=fine,
        in_specs=placed,
        out_specs=(P(TENSOR, DATA), P(TENSOR, DATA), P(DATA, TENSOR), P(DATA, TENSOR)),
        check_vma=False,
    )
```

```python
import jax
import jax.numpy as jnp
from jax import lax
from jax.experimental import pallas as pl
from jax.experimental.pallas import tpu as pltpu
from jax.sharding import Mesh, PartitionSpec as P

EPS = 1e-06
DATA = ("zl", "y", "c")
TENSOR = ("zh", "x")
SIZES = {"zl": 8, "y": 8, "c": 2, "zh": 2, "x": 4}
STEPS = (0, 1, 3, 2)
F32 = jnp.float32
BF16 = jnp.bfloat16


def dot(a, b, dims):
    return lax.dot_general(a, b, (dims, ((), ())), preferred_element_type=F32)


def exchange(blocks, axes):
    return lax.all_to_all(blocks, axes, 0, 0, tiled=True)


def spread(block, axes, count):
    return exchange(jnp.broadcast_to(block[None], (count, *block.shape)), axes)


def shifted(value, axis, by):
    size = SIZES[axis]
    return lax.ppermute(value, axis, [(i, (i + by) % size) for i in range(size)])


def flat(*sizes):
    return [lax.broadcasted_iota(jnp.int32, sizes, i).reshape(-1) for i in range(len(sizes))]


def pair_kernel(factors, own_ids, other_ids, mine, theirs, *refs):
    others, (mine_sum, theirs_sum, held) = refs[: len(STEPS)], refs[len(STEPS) :]
    size = others[0].shape[0]
    for i, block in enumerate(others):
        held[i * size : (i + 1) * size, :] = block[...]
    partners = held[...]
    for i, (rows, out) in enumerate(((mine, mine_sum), (theirs, theirs_sum))):
        logits = factors[0] * dot(rows[...], partners, ((1,), (1,))) + factors[1]
        target = jnp.where(own_ids[:, i : i + 1] == other_ids[0:1, :], 1.0, 0.0)
        crossed = own_ids[:, i + 2 : i + 3] != other_ids[1:2, :]
        coef = jnp.where(crossed, jax.nn.sigmoid(logits) - target, 0.0)
        out[...] = dot(coef.astype(BF16), partners, ((1,), (0,)))


def pair_sums(factors, own_ids, other_ids, mine, theirs, others):
    count, width = mine.shape
    partners = len(others) * others[0].shape[0]
    whole = pl.BlockSpec(memory_space=pltpu.VMEM)
    out = jax.ShapeDtypeStruct((count, width), F32)
    return pl.pallas_call(
        pair_kernel,
        out_shape=(out, out),
        in_specs=[pl.BlockSpec(memory_space=pltpu.SMEM)] + [whole] * (4 + len(others)),
        out_specs=(whole, whole),
        scratch_shapes=[pltpu.VMEM((partners, width), BF16)],
        compiler_params=pltpu.CompilerParams(vmem_limit_bytes=24 * 2**20),
        cost_estimate=pl.CostEstimate(
            flops=8 * count * partners * width,
            bytes_accessed=12 * count * width + 2 * partners * width,
            transcendentals=2 * count * partners,
        ),
    )(factors, own_ids, other_ids, mine, theirs, *others)


def local(image_features, text_features, image_weight, text_weight, log_scale, logit_bias):
    scale = jnp.exp(log_scale[0])
    bias = logit_bias[0]
    zl, y, c, zh, x = (lax.axis_index(axis) for axis in ("zl", "y", "c", "zh", "x"))
    rows, depth = image_features.shape
    width = image_weight.shape[1]
    own = rows // SIZES["x"]

    with jax.named_scope("embed"):
        parts = [
            dot(features, weight, ((1,), (0,))).astype(BF16).reshape(SIZES["x"], own, width)
            for features, weight in ((image_features, image_weight), (text_features, text_weight))
        ]
        parts = exchange(jnp.concatenate(parts, axis=1), "x")
        embed = jnp.sum(parts.astype(F32), axis=0)
        embed = embed + shifted(embed, "zh", 1)
        inverse = lax.rsqrt(jnp.sum(embed * embed, axis=-1, keepdims=True) + EPS)
        unit = embed * inverse
        vec = unit.astype(BF16)

    with jax.named_scope("gather_own"):
        mine = spread(vec, "y", SIZES["y"]).reshape(-1, width)
        theirs = shifted(mine, "c", 1)

    with jax.named_scope("gather_others"):
        half = own // 2
        column = lax.dynamic_slice_in_dim(vec.reshape(2, own, width), zh * half, half, axis=1)
        column = lax.all_gather(column.reshape(2 * half, width), "zl", tiled=True)
        others = [column] + [shifted(column, "x", by) for by in STEPS[1:]]

    with jax.named_scope("pairs"):
        hy, hkind, hrow = flat(SIZES["y"], 2, own)
        data = (zl * SIZES["y"] + hy) * 2
        row = x * own + hrow
        mine_id = (data + c) * rows + row
        theirs_id = (data + 1 - c) * rows + row
        ostep, ozl, okind, orow = flat(len(STEPS), SIZES["zl"], 2, half)
        step = jnp.where(ostep == 0, 0, jnp.where(ostep == 1, 1, jnp.where(ostep == 2, 3, 2)))
        place = (x - step + SIZES["x"]) % SIZES["x"]
        other_id = ((ozl * SIZES["y"] + y) * 2 + c) * rows + place * own + zh * half + orow
        kinds = jnp.stack([hkind, hkind], axis=1)
        own_ids = jnp.concatenate([jnp.stack([mine_id, theirs_id], axis=1), kinds], axis=1)
        other_ids = jnp.stack([other_id, okind])
        mine_sum, theirs_sum = pair_sums(
            jnp.stack([scale, bias]), own_ids, other_ids, mine, theirs, others
        )

    with jax.named_scope("reduce_pairs"):
        direction = mine_sum + shifted(theirs_sum, "c", 1)
        direction = exchange(direction.astype(BF16).reshape(SIZES["y"], 2 * own, width), "y")
        direction = jnp.sum(direction.astype(F32), axis=0)
        direction = scale * (direction + shifted(direction, "zh", 1))

    with jax.named_scope("back"):
        inner = jnp.sum(unit * direction, axis=-1, keepdims=True)
        back = (inverse * (direction - unit * inner)).astype(BF16)
        back = spread(back, "x", SIZES["x"]).reshape(-1, width)

    with jax.named_scope("feature_grad"):
        weights = jnp.concatenate([image_weight, text_weight])
        grads = dot(back, weights, ((1,), (1,))).reshape(SIZES["x"], 2, own, 2 * depth)
        image_feature_grad = grads[:, 0, :, :depth].reshape(rows, depth)
        text_feature_grad = grads[:, 1, :, depth:].reshape(rows, depth)

    with jax.named_scope("weight_grad"):
        blank = jnp.zeros((SIZES["x"], own, depth), BF16)
        features = jnp.concatenate(
            [
                jnp.concatenate([image_features.reshape(SIZES["x"], own, depth), blank], axis=2),
                jnp.concatenate([blank, text_features.reshape(SIZES["x"], own, depth)], axis=2),
            ],
            axis=1,
        ).reshape(2 * rows, 2 * depth)
        chips = SIZES["zl"] * SIZES["y"]
        share = width // (chips * 2)
        pc, pchip, pk = flat(2, chips, share)
        source = (pchip * 2 + jnp.where(pc == 0, c, 1 - c)) * share + pk
        order = lax.broadcasted_iota(jnp.int32, (width, width), 0) == source[None, :]
        sorted_back = dot(back, order.astype(BF16), ((1,), (0,))).astype(BF16)
        partial = dot(sorted_back, features, ((0,), (0,)))
        partial = partial[: width // 2] + shifted(partial[width // 2 :], "c", 1)
        partial = exchange(partial.astype(BF16).reshape(chips, share, 2 * depth), ("zl", "y"))
        total = jnp.sum(partial.astype(F32), axis=0).T

    return (total[:depth], total[depth:], image_feature_grad, text_feature_grad)


def solution(mesh):
    names = ("zl", "y", "c", "zh", "x")
    fine = Mesh(mesh.devices.reshape([SIZES[name] for name in names]), names)
    placed = (P(DATA, TENSOR), P(DATA, TENSOR), P(TENSOR, None), P(TENSOR, None), P(), P())
    return jax.shard_map(
        local,
        mesh=fine,
        in_specs=placed,
        out_specs=(P(TENSOR, DATA), P(TENSOR, DATA), P(DATA, TENSOR), P(DATA, TENSOR)),
        check_vma=False,
    )
```

```python
import jax
import jax.numpy as jnp
from jax import lax
from jax.experimental import pallas as pl
from jax.experimental.pallas import tpu as pltpu
from jax.sharding import Mesh, PartitionSpec as P

EPS = 1e-06
DATA = ("zl", "y", "c")
TENSOR = ("zh", "x")
SIZES = {"zl": 8, "y": 8, "c": 2, "zh": 2, "x": 4}
STEPS = (0, 1, 3, 2)
FIRST = (0, -1, 1)
GROUPS = FIRST + (-3, -4, -2, 3, 2)
RUN = 16
F32 = jnp.float32
BF16 = jnp.bfloat16


def dot(a, b, dims):
    return lax.dot_general(a, b, (dims, ((), ())), preferred_element_type=F32)


def exchange(blocks, axes):
    return lax.all_to_all(blocks, axes, 0, 0, tiled=True)


def spread(block, axes, count):
    return exchange(jnp.broadcast_to(block[None], (count, *block.shape)), axes)


def shifted(value, axis, by):
    size = SIZES[axis]
    return lax.ppermute(value, axis, [(i, (i + by) % size) for i in range(size)])


def along_z(value, by):
    size = SIZES["zh"] * SIZES["zl"]
    place = [(z % SIZES["zl"]) * SIZES["zh"] + z // SIZES["zl"] for z in range(size)]
    pairs = [(place[z], place[(z + by) % size]) for z in range(size)]
    return lax.ppermute(value, ("zl", "zh"), pairs)


def flat(*sizes):
    return [lax.broadcasted_iota(jnp.int32, sizes, i).reshape(-1) for i in range(len(sizes))]


def pair_kernel(factors, own_ids, other_ids, mine, theirs, *refs):
    blocks, (mine_sum, theirs_sum, held, partners) = refs[: len(STEPS)], refs[len(STEPS) :]
    run = RUN
    for kind in range(2):
        for target, sources in ((held, (mine, theirs)), (partners, blocks)):
            at = 0
            for source in sources:
                for start in range(kind * run, source.shape[0], 2 * run):
                    target[kind, at : at + run, :] = source[start : start + run, :]
                    at += run
    matched = own_ids[...] == other_ids[...]
    count = held.shape[1] // 2
    for kind in range(2):
        other = partners[1 - kind]
        logits = factors[0] * dot(held[kind], other, ((1,), (1,))) + factors[1]
        coef = jax.nn.sigmoid(logits) - jnp.where(matched, 1.0, 0.0)
        total = dot(coef.astype(BF16), other, ((1,), (0,)))
        for part, out in ((total[:count], mine_sum), (total[count:], theirs_sum)):
            for at in range(0, count, run):
                start = 2 * at + kind * run
                out[start : start + run, :] = part[at : at + run]


def pair_sums(factors, own_ids, other_ids, mine, theirs, others):
    count, width = mine.shape
    partners = len(others) * others[0].shape[0]
    whole = pl.BlockSpec(memory_space=pltpu.VMEM)
    out = jax.ShapeDtypeStruct((count, width), F32)
    return pl.pallas_call(
        pair_kernel,
        out_shape=(out, out),
        in_specs=[pl.BlockSpec(memory_space=pltpu.SMEM)] + [whole] * (4 + len(others)),
        out_specs=(whole, whole),
        scratch_shapes=[
            pltpu.VMEM((2, count, width), BF16),
            pltpu.VMEM((2, partners // 2, width), BF16),
        ],
        compiler_params=pltpu.CompilerParams(vmem_limit_bytes=28 * 2**20),
        cost_estimate=pl.CostEstimate(
            flops=4 * count * partners * width,
            bytes_accessed=12 * count * width + 2 * partners * width,
            transcendentals=count * partners,
        ),
    )(factors, own_ids, other_ids, mine, theirs, *others)


def local(image_features, text_features, image_weight, text_weight, log_scale, logit_bias):
    scale = jnp.exp(log_scale[0])
    bias = logit_bias[0]
    zl, y, c, x = (lax.axis_index(axis) for axis in ("zl", "y", "c", "x"))
    rows, depth = image_features.shape
    width = image_weight.shape[1]
    own = rows // SIZES["x"]

    with jax.named_scope("embed"):
        parts = [
            dot(features, weight, ((1,), (0,))).astype(BF16).reshape(SIZES["x"], own, width)
            for features, weight in ((image_features, image_weight), (text_features, text_weight))
        ]
        parts = exchange(jnp.concatenate(parts, axis=1), "x")
        embed = jnp.sum(parts.astype(F32), axis=0)
        embed = embed + shifted(embed, "zh", 1)
        inverse = lax.rsqrt(jnp.sum(embed * embed, axis=-1, keepdims=True) + EPS)
        unit = embed * inverse
        vec = unit.astype(BF16)

    with jax.named_scope("gather_own"):
        mine = spread(vec, "y", SIZES["y"]).reshape(-1, width)
        theirs = shifted(mine, "c", 1)

    with jax.named_scope("gather_others"):
        behind, ahead = along_z(vec, 1), along_z(vec, -1)
        near = jnp.concatenate([vec, behind, ahead])
        far = [along_z(near, 3), along_z(jnp.concatenate([vec, behind]), -3)]
        column = jnp.concatenate([near] + far)
        others = [column] + [shifted(column, "x", by) for by in STEPS[1:]]

    with jax.named_scope("pairs"):
        hc, hy, hrow = flat(2, SIZES["y"], own)
        held_data = (zl * SIZES["y"] + hy) * 2 + jnp.where(hc == 0, c, 1 - c)
        held_id = held_data * rows + x * own + hrow
        orow = lax.iota(jnp.int32, own)
        other_id = []
        for step in STEPS:
            for group in GROUPS:
                data = ((zl + group + SIZES["zl"]) % SIZES["zl"] * SIZES["y"] + y) * 2 + c
                place = (x - step + SIZES["x"]) % SIZES["x"]
                other_id.append(data * rows + place * own + orow)
        mine_sum, theirs_sum = pair_sums(
            jnp.stack([scale, bias]),
            held_id[:, None],
            jnp.concatenate(other_id)[None, :],
            mine,
            theirs,
            others,
        )

    with jax.named_scope("reduce_pairs"):
        direction = mine_sum + shifted(theirs_sum, "c", 1)
        direction = exchange(direction.astype(BF16).reshape(SIZES["y"], 2 * own, width), "y")
        direction = scale * jnp.sum(direction.astype(F32), axis=0)

    with jax.named_scope("back"):
        inner = jnp.sum(unit * direction, axis=-1, keepdims=True)
        back = (inverse * (direction - unit * inner)).astype(BF16)
        back = spread(back, "x", SIZES["x"]).reshape(-1, width)

    with jax.named_scope("feature_grad"):
        weights = jnp.concatenate([image_weight, text_weight])
        grads = dot(back, weights, ((1,), (1,))).reshape(SIZES["x"], 2, own, 2 * depth)
        image_feature_grad = grads[:, 0, :, :depth].reshape(rows, depth)
        text_feature_grad = grads[:, 1, :, depth:].reshape(rows, depth)

    with jax.named_scope("weight_grad"):
        blank = jnp.zeros((SIZES["x"], own, depth), BF16)
        features = jnp.concatenate(
            [
                jnp.concatenate([image_features.reshape(SIZES["x"], own, depth), blank], axis=2),
                jnp.concatenate([blank, text_features.reshape(SIZES["x"], own, depth)], axis=2),
            ],
            axis=1,
        ).reshape(2 * rows, 2 * depth)
        chips = SIZES["zl"] * SIZES["y"]
        share = width // (chips * 2)
        pc, pchip, pk = flat(2, chips, share)
        source = (pchip * 2 + jnp.where(pc == 0, c, 1 - c)) * share + pk
        order = lax.broadcasted_iota(jnp.int32, (width, width), 0) == source[None, :]
        sorted_back = dot(back, order.astype(BF16), ((1,), (0,))).astype(BF16)
        partial = dot(sorted_back, features, ((0,), (0,)))
        partial = partial[: width // 2] + shifted(partial[width // 2 :], "c", 1)
        partial = exchange(partial.astype(BF16).reshape(chips, share, 2 * depth), ("zl", "y"))
        total = jnp.sum(partial.astype(F32), axis=0).T

    return (total[:depth], total[depth:], image_feature_grad, text_feature_grad)


def solution(mesh):
    names = ("zl", "y", "c", "zh", "x")
    fine = Mesh(mesh.devices.reshape([SIZES[name] for name in names]), names)
    placed = (P(DATA, TENSOR), P(DATA, TENSOR), P(TENSOR, None), P(TENSOR, None), P(), P())
    return jax.shard_map(
        local,
        mesh=fine,
        in_specs=placed,
        out_specs=(P(TENSOR, DATA), P(TENSOR, DATA), P(DATA, TENSOR), P(DATA, TENSOR)),
        check_vma=False,
    )
```

```python
import jax
import jax.numpy as jnp
from jax import lax
from jax.experimental import pallas as pl
from jax.experimental.pallas import tpu as pltpu
from jax.sharding import Mesh, PartitionSpec as P

EPS = 1e-06
DATA = ("zl", "y", "c")
TENSOR = ("zh", "x")
SIZES = {"zl": 8, "y": 8, "c": 2, "zh": 2, "x": 4}
STEPS = (0, 1, 3, 2)
NEAR = (0, -1, 1)
FAR = (-3, -4, -2, 3, 2)
RUN = 16
F32 = jnp.float32
BF16 = jnp.bfloat16


def dot(a, b, dims):
    return lax.dot_general(a, b, (dims, ((), ())), preferred_element_type=F32)


def exchange(blocks, axes):
    return lax.all_to_all(blocks, axes, 0, 0, tiled=True)


def spread(block, axes, count):
    return exchange(jnp.broadcast_to(block[None], (count, *block.shape)), axes)


def shifted(value, axis, by):
    size = SIZES[axis]
    return lax.ppermute(value, axis, [(i, (i + by) % size) for i in range(size)])


def along_z(value, by):
    size = SIZES["zh"] * SIZES["zl"]
    place = [(z % SIZES["zl"]) * SIZES["zh"] + z // SIZES["zl"] for z in range(size)]
    pairs = [(place[z], place[(z + by) % size]) for z in range(size)]
    return lax.ppermute(value, ("zl", "zh"), pairs)


def flat(*sizes):
    return [lax.broadcasted_iota(jnp.int32, sizes, i).reshape(-1) for i in range(len(sizes))]


def pair_kernel(factors, own_ids, other_ids, mine, theirs, *refs):
    blocks, (mine_sum, theirs_sum, held, partners) = refs[:-4], refs[-4:]
    run = RUN
    for kind in range(2):
        for target, sources in ((held, (mine, theirs)), (partners, blocks)):
            at = 0
            for source in sources:
                for start in range(kind * run, source.shape[0], 2 * run):
                    target[kind, at : at + run, :] = source[start : start + run, :]
                    at += run
    matched = own_ids[...] == other_ids[...]
    count = held.shape[1] // 2
    for kind in range(2):
        other = partners[1 - kind]
        logits = factors[0] * dot(held[kind], other, ((1,), (1,))) + factors[1]
        coef = jax.nn.sigmoid(logits) - jnp.where(matched, 1.0, 0.0)
        total = dot(coef.astype(BF16), other, ((1,), (0,)))
        for part, out in ((total[:count], mine_sum), (total[count:], theirs_sum)):
            for at in range(0, count, run):
                start = 2 * at + kind * run
                out[start : start + run, :] = part[at : at + run]


def pair_sums(factors, own_ids, other_ids, mine, theirs, others):
    count, width = mine.shape
    partners = sum(block.shape[0] for block in others)
    whole = pl.BlockSpec(memory_space=pltpu.VMEM)
    out = jax.ShapeDtypeStruct((count, width), F32)
    return pl.pallas_call(
        pair_kernel,
        out_shape=(out, out),
        in_specs=[pl.BlockSpec(memory_space=pltpu.SMEM)] + [whole] * (4 + len(others)),
        out_specs=(whole, whole),
        scratch_shapes=[
            pltpu.VMEM((2, count, width), BF16),
            pltpu.VMEM((2, partners // 2, width), BF16),
        ],
        compiler_params=pltpu.CompilerParams(vmem_limit_bytes=28 * 2**20),
        cost_estimate=pl.CostEstimate(
            flops=4 * count * partners * width,
            bytes_accessed=12 * count * width + 2 * partners * width,
            transcendentals=count * partners,
        ),
    )(factors, own_ids, other_ids, mine, theirs, *others)


def local(image_features, text_features, image_weight, text_weight, log_scale, logit_bias):
    scale = jnp.exp(log_scale[0])
    bias = logit_bias[0]
    zl, y, c, x = (lax.axis_index(axis) for axis in ("zl", "y", "c", "x"))
    rows, depth = image_features.shape
    width = image_weight.shape[1]
    own = rows // SIZES["x"]

    with jax.named_scope("embed"):
        parts = [
            dot(features, weight, ((1,), (0,))).astype(BF16).reshape(SIZES["x"], own, width)
            for features, weight in ((image_features, image_weight), (text_features, text_weight))
        ]
        parts = exchange(jnp.concatenate(parts, axis=1), "x")
        embed = jnp.sum(parts.astype(F32), axis=0)
        embed = embed + shifted(embed, "zh", 1)
        inverse = lax.rsqrt(jnp.sum(embed * embed, axis=-1, keepdims=True) + EPS)
        unit = embed * inverse
        vec = unit.astype(BF16)

    with jax.named_scope("gather_others"):
        behind, ahead = along_z(vec, 1), along_z(vec, -1)
        near = jnp.concatenate([vec, behind, ahead])
        far = [along_z(near, 3), along_z(jnp.concatenate([vec, behind]), -3)]
        near_moved = [shifted(near, "x", by) for by in STEPS[1:]]
        vec, near_moved[0] = lax.optimization_barrier((vec, near_moved[0]))
        far = jnp.concatenate(far)
        far_moved = [shifted(far, "x", by) for by in STEPS[1:]]
        others = [near, *near_moved, far, *far_moved]

    with jax.named_scope("gather_own"):
        mine = spread(vec, "y", SIZES["y"]).reshape(-1, width)
        theirs = shifted(mine, "c", 1)

    with jax.named_scope("pairs"):
        hc, hy, hrow = flat(2, SIZES["y"], own)
        held_data = (zl * SIZES["y"] + hy) * 2 + jnp.where(hc == 0, c, 1 - c)
        held_id = held_data * rows + x * own + hrow
        orow = lax.iota(jnp.int32, own)
        other_id = []
        for groups in (NEAR, FAR):
            for step, group in ((step, group) for step in STEPS for group in groups):
                data = ((zl + group + SIZES["zl"]) % SIZES["zl"] * SIZES["y"] + y) * 2 + c
                place = (x - step + SIZES["x"]) % SIZES["x"]
                other_id.append(data * rows + place * own + orow)
        mine_sum, theirs_sum = pair_sums(
            jnp.stack([scale, bias]),
            held_id[:, None],
            jnp.concatenate(other_id)[None, :],
            mine,
            theirs,
            others,
        )

    with jax.named_scope("reduce_pairs"):
        direction = mine_sum + shifted(theirs_sum, "c", 1)
        direction = exchange(direction.astype(BF16).reshape(SIZES["y"], 2 * own, width), "y")
        direction = scale * jnp.sum(direction.astype(F32), axis=0)

    with jax.named_scope("back"):
        inner = jnp.sum(unit * direction, axis=-1, keepdims=True)
        back = (inverse * (direction - unit * inner)).astype(BF16)
        back = spread(back, "x", SIZES["x"]).reshape(-1, width)

    with jax.named_scope("feature_grad"):
        weights = jnp.concatenate([image_weight, text_weight])
        grads = dot(back, weights, ((1,), (1,))).reshape(SIZES["x"], 2, own, 2 * depth)
        image_feature_grad = grads[:, 0, :, :depth].reshape(rows, depth)
        text_feature_grad = grads[:, 1, :, depth:].reshape(rows, depth)

    with jax.named_scope("weight_grad"):
        blank = jnp.zeros((SIZES["x"], own, depth), BF16)
        features = jnp.concatenate(
            [
                jnp.concatenate([image_features.reshape(SIZES["x"], own, depth), blank], axis=2),
                jnp.concatenate([blank, text_features.reshape(SIZES["x"], own, depth)], axis=2),
            ],
            axis=1,
        ).reshape(2 * rows, 2 * depth)
        chips = SIZES["zl"] * SIZES["y"]
        share = width // (chips * 2)
        pc, pchip, pk = flat(2, chips, share)
        source = (pchip * 2 + jnp.where(pc == 0, c, 1 - c)) * share + pk
        order = lax.broadcasted_iota(jnp.int32, (width, width), 0) == source[None, :]
        sorted_back = dot(back, order.astype(BF16), ((1,), (0,))).astype(BF16)
        partial = dot(sorted_back, features, ((0,), (0,)))
        partial = partial[: width // 2] + shifted(partial[width // 2 :], "c", 1)
        partial = exchange(partial.astype(BF16).reshape(chips, share, 2 * depth), ("zl", "y"))
        total = jnp.sum(partial.astype(F32), axis=0).T

    return (total[:depth], total[depth:], image_feature_grad, text_feature_grad)


def solution(mesh):
    names = ("zl", "y", "c", "zh", "x")
    fine = Mesh(mesh.devices.reshape([SIZES[name] for name in names]), names)
    placed = (P(DATA, TENSOR), P(DATA, TENSOR), P(TENSOR, None), P(TENSOR, None), P(), P())
    return jax.shard_map(
        local,
        mesh=fine,
        in_specs=placed,
        out_specs=(P(TENSOR, DATA), P(TENSOR, DATA), P(DATA, TENSOR), P(DATA, TENSOR)),
        check_vma=False,
    )
```

```python
import jax
import jax.numpy as jnp
from jax import lax
from jax.experimental import pallas as pl
from jax.experimental.pallas import tpu as pltpu
from jax.sharding import Mesh, PartitionSpec as P

EPS = 1e-06
DATA = ("zl", "y", "c")
TENSOR = ("zh", "x")
SIZES = {"zl": 8, "y": 8, "c": 2, "zh": 2, "x": 4}
STEPS = (0, 1, 3, 2)
GROUPS = (0, -4, -1, -5, 1, -3, -2, -6)
RUN = 16
F32 = jnp.float32
BF16 = jnp.bfloat16


def dot(a, b, dims):
    return lax.dot_general(a, b, (dims, ((), ())), preferred_element_type=F32)


def exchange(blocks, axes):
    return lax.all_to_all(blocks, axes, 0, 0, tiled=True)


def spread(block, axes, count):
    return exchange(jnp.broadcast_to(block[None], (count, *block.shape)), axes)


def shifted(value, axis, by):
    size = SIZES[axis]
    return lax.ppermute(value, axis, [(i, (i + by) % size) for i in range(size)])


def along_z(value, by):
    size = SIZES["zh"] * SIZES["zl"]
    place = [(z % SIZES["zl"]) * SIZES["zh"] + z // SIZES["zl"] for z in range(size)]
    pairs = [(place[z], place[(z + by) % size]) for z in range(size)]
    return lax.ppermute(value, ("zl", "zh"), pairs)


def flat(*sizes):
    return [lax.broadcasted_iota(jnp.int32, sizes, i).reshape(-1) for i in range(len(sizes))]


def pair_kernel(factors, own_ids, other_ids, mine, theirs, *refs):
    blocks, (mine_sum, theirs_sum, held, partners) = refs[: len(STEPS)], refs[len(STEPS) :]
    run = RUN
    for kind in range(2):
        for target, sources in ((held, (mine, theirs)), (partners, blocks)):
            at = 0
            for source in sources:
                for start in range(kind * run, source.shape[0], 2 * run):
                    target[kind, at : at + run, :] = source[start : start + run, :]
                    at += run
    matched = own_ids[...] == other_ids[...]
    count = held.shape[1] // 2
    for kind in range(2):
        other = partners[1 - kind]
        logits = factors[0] * dot(held[kind], other, ((1,), (1,))) + factors[1]
        coef = jax.nn.sigmoid(logits) - jnp.where(matched, 1.0, 0.0)
        total = dot(coef.astype(BF16), other, ((1,), (0,)))
        for part, out in ((total[:count], mine_sum), (total[count:], theirs_sum)):
            for at in range(0, count, run):
                start = 2 * at + kind * run
                out[start : start + run, :] = part[at : at + run]


def pair_sums(factors, own_ids, other_ids, mine, theirs, others):
    count, width = mine.shape
    partners = len(others) * others[0].shape[0]
    whole = pl.BlockSpec(memory_space=pltpu.VMEM)
    out = jax.ShapeDtypeStruct((count, width), F32)
    return pl.pallas_call(
        pair_kernel,
        out_shape=(out, out),
        in_specs=[pl.BlockSpec(memory_space=pltpu.SMEM)] + [whole] * (4 + len(others)),
        out_specs=(whole, whole),
        scratch_shapes=[
            pltpu.VMEM((2, count, width), BF16),
            pltpu.VMEM((2, partners // 2, width), BF16),
        ],
        compiler_params=pltpu.CompilerParams(vmem_limit_bytes=28 * 2**20),
        cost_estimate=pl.CostEstimate(
            flops=4 * count * partners * width,
            bytes_accessed=12 * count * width + 2 * partners * width,
            transcendentals=count * partners,
        ),
    )(factors, own_ids, other_ids, mine, theirs, *others)


def local(image_features, text_features, image_weight, text_weight, log_scale, logit_bias):
    scale = jnp.exp(log_scale[0])
    bias = logit_bias[0]
    zl, y, c, x = (lax.axis_index(axis) for axis in ("zl", "y", "c", "x"))
    rows, depth = image_features.shape
    width = image_weight.shape[1]
    own = rows // SIZES["x"]

    with jax.named_scope("embed"):
        parts = [
            dot(features, weight, ((1,), (0,))).astype(BF16).reshape(SIZES["x"], own, width)
            for features, weight in ((image_features, image_weight), (text_features, text_weight))
        ]
        parts = exchange(jnp.concatenate(parts, axis=1), "x")
        embed = jnp.sum(parts.astype(F32), axis=0)
        embed = embed + shifted(embed, "zh", 1)
        inverse = lax.rsqrt(jnp.sum(embed * embed, axis=-1, keepdims=True) + EPS)
        unit = embed * inverse
        vec = unit.astype(BF16)

    with jax.named_scope("gather_own"):
        mine = spread(vec, "y", SIZES["y"]).reshape(-1, width)
        theirs = shifted(mine, "c", 1)

    with jax.named_scope("gather_others"):
        pair = jnp.concatenate([vec, along_z(vec, 4)])
        column = jnp.concatenate([pair] + [along_z(pair, by) for by in (1, -1, 2)])
        others = [column] + [shifted(column, "x", by) for by in STEPS[1:]]

    with jax.named_scope("pairs"):
        hc, hy, hrow = flat(2, SIZES["y"], own)
        held_data = (zl * SIZES["y"] + hy) * 2 + jnp.where(hc == 0, c, 1 - c)
        held_id = held_data * rows + x * own + hrow
        orow = lax.iota(jnp.int32, own)
        other_id = []
        for step in STEPS:
            for group in GROUPS:
                data = ((zl + group + SIZES["zl"]) % SIZES["zl"] * SIZES["y"] + y) * 2 + c
                place = (x - step + SIZES["x"]) % SIZES["x"]
                other_id.append(data * rows + place * own + orow)
        mine_sum, theirs_sum = pair_sums(
            jnp.stack([scale, bias]),
            held_id[:, None],
            jnp.concatenate(other_id)[None, :],
            mine,
            theirs,
            others,
        )

    with jax.named_scope("reduce_pairs"):
        direction = mine_sum + shifted(theirs_sum, "c", 1)
        direction = exchange(direction.astype(BF16).reshape(SIZES["y"], 2 * own, width), "y")
        direction = scale * jnp.sum(direction.astype(F32), axis=0)

    with jax.named_scope("back"):
        inner = jnp.sum(unit * direction, axis=-1, keepdims=True)
        back = (inverse * (direction - unit * inner)).astype(BF16)
        back = spread(back, "x", SIZES["x"]).reshape(-1, width)

    with jax.named_scope("feature_grad"):
        weights = jnp.concatenate([image_weight, text_weight])
        grads = dot(back, weights, ((1,), (1,))).reshape(SIZES["x"], 2, own, 2 * depth)
        image_feature_grad = grads[:, 0, :, :depth].reshape(rows, depth)
        text_feature_grad = grads[:, 1, :, depth:].reshape(rows, depth)

    with jax.named_scope("weight_grad"):
        blank = jnp.zeros((SIZES["x"], own, depth), BF16)
        features = jnp.concatenate(
            [
                jnp.concatenate([image_features.reshape(SIZES["x"], own, depth), blank], axis=2),
                jnp.concatenate([blank, text_features.reshape(SIZES["x"], own, depth)], axis=2),
            ],
            axis=1,
        ).reshape(2 * rows, 2 * depth)
        chips = SIZES["zl"] * SIZES["y"]
        share = width // (chips * 2)
        pc, pchip, pk = flat(2, chips, share)
        source = (pchip * 2 + jnp.where(pc == 0, c, 1 - c)) * share + pk
        order = lax.broadcasted_iota(jnp.int32, (width, width), 0) == source[None, :]
        sorted_back = dot(back, order.astype(BF16), ((1,), (0,))).astype(BF16)
        partial = dot(sorted_back, features, ((0,), (0,)))
        partial = partial[: width // 2] + shifted(partial[width // 2 :], "c", 1)
        partial = exchange(partial.astype(BF16).reshape(chips, share, 2 * depth), ("zl", "y"))
        total = jnp.sum(partial.astype(F32), axis=0).T

    return (total[:depth], total[depth:], image_feature_grad, text_feature_grad)


def solution(mesh):
    names = ("zl", "y", "c", "zh", "x")
    fine = Mesh(mesh.devices.reshape([SIZES[name] for name in names]), names)
    placed = (P(DATA, TENSOR), P(DATA, TENSOR), P(TENSOR, None), P(TENSOR, None), P(), P())
    return jax.shard_map(
        local,
        mesh=fine,
        in_specs=placed,
        out_specs=(P(TENSOR, DATA), P(TENSOR, DATA), P(DATA, TENSOR), P(DATA, TENSOR)),
        check_vma=False,
    )
```

```python
import jax
import jax.numpy as jnp
from jax import lax
from jax.experimental import pallas as pl
from jax.experimental.pallas import tpu as pltpu
from jax.sharding import Mesh, PartitionSpec as P

EPS = 1e-06
DATA = ("zl", "y", "c")
TENSOR = ("zh", "x")
SIZES = {"zl": 8, "y": 8, "c": 2, "zh": 2, "x": 4}
STEPS = (0, 1, 3, 2)
GROUPS = (0, -4, -1, -5, 1, -3, -2, -6)
RUN = 16
F32 = jnp.float32
BF16 = jnp.bfloat16


def dot(a, b, dims):
    return lax.dot_general(a, b, (dims, ((), ())), preferred_element_type=F32)


def exchange(blocks, axes):
    return lax.all_to_all(blocks, axes, 0, 0, tiled=True)


def spread(block, axes, count):
    return exchange(jnp.broadcast_to(block[None], (count, *block.shape)), axes)


def shifted(value, axis, by):
    size = SIZES[axis]
    return lax.ppermute(value, axis, [(i, (i + by) % size) for i in range(size)])


def along_z(value, by):
    size = SIZES["zh"] * SIZES["zl"]
    place = [(z % SIZES["zl"]) * SIZES["zh"] + z // SIZES["zl"] for z in range(size)]
    pairs = [(place[z], place[(z + by) % size]) for z in range(size)]
    return lax.ppermute(value, ("zl", "zh"), pairs)


def along_y(value, by):
    return shifted(value, "y", by)


def ring_gather(block, step):
    pair = jnp.concatenate([block, step(block, 4)])
    return jnp.concatenate([pair] + [step(pair, by) for by in (1, -1, 2)])


def flat(*sizes):
    return [lax.broadcasted_iota(jnp.int32, sizes, i).reshape(-1) for i in range(len(sizes))]


def pair_kernel(factors, places, own_ids, other_ids, mine, theirs, *refs):
    blocks, (mine_sum, theirs_sum, held, partners) = refs[: len(STEPS)], refs[len(STEPS) :]
    run = RUN
    for kind in range(2):
        for target, sources in ((held, (mine, theirs)), (partners, blocks)):
            at = 0
            for source in sources:
                for start in range(kind * run, source.shape[0], 2 * run):
                    target[kind, at : at + run, :] = source[start : start + run, :]
                    at += run
    matched = own_ids[...] == other_ids[...]
    count = held.shape[1] // 2
    for kind in range(2):
        other = partners[1 - kind]
        logits = factors[0] * dot(held[kind], other, ((1,), (1,))) + factors[1]
        coef = jax.nn.sigmoid(logits) - jnp.where(matched, 1.0, 0.0)
        total = dot(coef.astype(BF16), other, ((1,), (0,)))
        for part, out in ((total[:count], mine_sum), (total[count:], theirs_sum)):
            for group in range(len(GROUPS)):
                start = pl.multiple_of((2 * places[group] + kind) * run, run)
                out[pl.ds(start, run), :] = part[group * run : (group + 1) * run]


def pair_sums(factors, places, own_ids, other_ids, mine, theirs, others):
    count, width = mine.shape
    partners = len(others) * others[0].shape[0]
    whole = pl.BlockSpec(memory_space=pltpu.VMEM)
    out = jax.ShapeDtypeStruct((count, width), F32)
    return pl.pallas_call(
        pair_kernel,
        out_shape=(out, out),
        in_specs=[pl.BlockSpec(memory_space=pltpu.SMEM)] * 2 + [whole] * (4 + len(others)),
        out_specs=(whole, whole),
        scratch_shapes=[
            pltpu.VMEM((2, count, width), BF16),
            pltpu.VMEM((2, partners // 2, width), BF16),
        ],
        compiler_params=pltpu.CompilerParams(vmem_limit_bytes=28 * 2**20),
        cost_estimate=pl.CostEstimate(
            flops=4 * count * partners * width,
            bytes_accessed=12 * count * width + 2 * partners * width,
            transcendentals=count * partners,
        ),
    )(factors, places, own_ids, other_ids, mine, theirs, *others)


def local(image_features, text_features, image_weight, text_weight, log_scale, logit_bias):
    scale = jnp.exp(log_scale[0])
    bias = logit_bias[0]
    zl, y, c, x = (lax.axis_index(axis) for axis in ("zl", "y", "c", "x"))
    rows, depth = image_features.shape
    width = image_weight.shape[1]
    own = rows // SIZES["x"]

    with jax.named_scope("embed"):
        parts = [
            dot(features, weight, ((1,), (0,))).astype(BF16).reshape(SIZES["x"], own, width)
            for features, weight in ((image_features, image_weight), (text_features, text_weight))
        ]
        parts = exchange(jnp.concatenate(parts, axis=1), "x")
        embed = jnp.sum(parts.astype(F32), axis=0)
        embed = embed + shifted(embed, "zh", 1)
        inverse = lax.rsqrt(jnp.sum(embed * embed, axis=-1, keepdims=True) + EPS)
        unit = embed * inverse
        vec = unit.astype(BF16)

    with jax.named_scope("gather_own"):
        mine = ring_gather(vec, along_y)
        theirs = shifted(mine, "c", 1)

    with jax.named_scope("gather_others"):
        column = ring_gather(vec, along_z)
        others = [column] + [shifted(column, "x", by) for by in STEPS[1:]]

    with jax.named_scope("pairs"):
        orow = lax.iota(jnp.int32, own)
        places = [(y + group + SIZES["y"]) % SIZES["y"] for group in GROUPS]
        held_id = []
        for core in (c, 1 - c):
            for place in places:
                data = (zl * SIZES["y"] + place) * 2 + core
                held_id.append(data * rows + x * own + orow)
        other_id = []
        for step in STEPS:
            for group in GROUPS:
                data = ((zl + group + SIZES["zl"]) % SIZES["zl"] * SIZES["y"] + y) * 2 + c
                place = (x - step + SIZES["x"]) % SIZES["x"]
                other_id.append(data * rows + place * own + orow)
        mine_sum, theirs_sum = pair_sums(
            jnp.stack([scale, bias]),
            jnp.stack(places),
            jnp.concatenate(held_id)[:, None],
            jnp.concatenate(other_id)[None, :],
            mine,
            theirs,
            others,
        )

    with jax.named_scope("reduce_pairs"):
        direction = mine_sum + shifted(theirs_sum, "c", 1)
        direction = exchange(direction.astype(BF16).reshape(SIZES["y"], 2 * own, width), "y")
        direction = scale * jnp.sum(direction.astype(F32), axis=0)

    with jax.named_scope("back"):
        inner = jnp.sum(unit * direction, axis=-1, keepdims=True)
        back = (inverse * (direction - unit * inner)).astype(BF16)
        back = spread(back, "x", SIZES["x"]).reshape(-1, width)

    with jax.named_scope("feature_grad"):
        weights = jnp.concatenate([image_weight, text_weight])
        grads = dot(back, weights, ((1,), (1,))).reshape(SIZES["x"], 2, own, 2 * depth)
        image_feature_grad = grads[:, 0, :, :depth].reshape(rows, depth)
        text_feature_grad = grads[:, 1, :, depth:].reshape(rows, depth)

    with jax.named_scope("weight_grad"):
        blank = jnp.zeros((SIZES["x"], own, depth), BF16)
        features = jnp.concatenate(
            [
                jnp.concatenate([image_features.reshape(SIZES["x"], own, depth), blank], axis=2),
                jnp.concatenate([blank, text_features.reshape(SIZES["x"], own, depth)], axis=2),
            ],
            axis=1,
        ).reshape(2 * rows, 2 * depth)
        chips = SIZES["zl"] * SIZES["y"]
        share = width // (chips * 2)
        pc, pchip, pk = flat(2, chips, share)
        source = (pchip * 2 + jnp.where(pc == 0, c, 1 - c)) * share + pk
        order = lax.broadcasted_iota(jnp.int32, (width, width), 0) == source[None, :]
        sorted_back = dot(back, order.astype(BF16), ((1,), (0,))).astype(BF16)
        partial = dot(sorted_back, features, ((0,), (0,)))
        partial = partial[: width // 2] + shifted(partial[width // 2 :], "c", 1)
        partial = exchange(partial.astype(BF16).reshape(chips, share, 2 * depth), ("zl", "y"))
        total = jnp.sum(partial.astype(F32), axis=0).T

    return (total[:depth], total[depth:], image_feature_grad, text_feature_grad)


def solution(mesh):
    names = ("zl", "y", "c", "zh", "x")
    fine = Mesh(mesh.devices.reshape([SIZES[name] for name in names]), names)
    placed = (P(DATA, TENSOR), P(DATA, TENSOR), P(TENSOR, None), P(TENSOR, None), P(), P())
    return jax.shard_map(
        local,
        mesh=fine,
        in_specs=placed,
        out_specs=(P(TENSOR, DATA), P(TENSOR, DATA), P(DATA, TENSOR), P(DATA, TENSOR)),
        check_vma=False,
    )
```

```python
import jax
import jax.numpy as jnp
from jax import lax
from jax.experimental import pallas as pl
from jax.experimental.pallas import tpu as pltpu
from jax.sharding import Mesh, PartitionSpec as P

EPS = 1e-06
DATA = ("zl", "y", "c")
TENSOR = ("zh", "x")
SIZES = {"zl": 8, "y": 8, "c": 2, "zh": 2, "x": 4}
STEPS = (0, 1, 3, 2)
GROUPS = (0, -4, -1, -5, 1, -3, -2, -6)
F32 = jnp.float32
BF16 = jnp.bfloat16


def dot(a, b, dims):
    return lax.dot_general(a, b, (dims, ((), ())), preferred_element_type=F32)


def exchange(blocks, axes):
    return lax.all_to_all(blocks, axes, 0, 0, tiled=True)


def spread(block, axes, count):
    return exchange(jnp.broadcast_to(block[None], (count, *block.shape)), axes)


def shifted(value, axis, by):
    size = SIZES[axis]
    return lax.ppermute(value, axis, [(i, (i + by) % size) for i in range(size)])


def along_z(value, by):
    size = SIZES["zh"] * SIZES["zl"]
    place = [(z % SIZES["zl"]) * SIZES["zh"] + z // SIZES["zl"] for z in range(size)]
    pairs = [(place[z], place[(z + by) % size]) for z in range(size)]
    return lax.ppermute(value, ("zl", "zh"), pairs)


def flat(*sizes):
    return [lax.broadcasted_iota(jnp.int32, sizes, i).reshape(-1) for i in range(len(sizes))]


def pair_kernel(factors, own_ids, other_ids, mine, theirs, *refs):
    blocks, (mine_sum, theirs_sum, held, partners) = refs[: len(STEPS)], refs[len(STEPS) :]
    for target, sources in ((held, (mine, theirs)), (partners, blocks)):
        size = sources[0].shape[0]
        for i, source in enumerate(sources):
            target[i * size : (i + 1) * size, :] = source[...]
    other = partners[...]
    logits = factors[0] * dot(held[...], other, ((1,), (1,))) + factors[1]
    coef = jax.nn.sigmoid(logits) - jnp.where(own_ids[...] == other_ids[...], 1.0, 0.0)
    total = dot(coef.astype(BF16), other, ((1,), (0,)))
    count = mine.shape[0]
    mine_sum[...] = total[:count]
    theirs_sum[...] = total[count:]


def pair_sums(factors, own_ids, other_ids, mine, theirs, others):
    count, width = mine.shape
    partners = len(others) * others[0].shape[0]
    whole = pl.BlockSpec(memory_space=pltpu.VMEM)
    out = jax.ShapeDtypeStruct((count, width), F32)
    return pl.pallas_call(
        pair_kernel,
        out_shape=(out, out),
        in_specs=[pl.BlockSpec(memory_space=pltpu.SMEM)] + [whole] * (4 + len(others)),
        out_specs=(whole, whole),
        scratch_shapes=[pltpu.VMEM((2 * count, width), BF16), pltpu.VMEM((partners, width), BF16)],
        compiler_params=pltpu.CompilerParams(vmem_limit_bytes=24 * 2**20),
        cost_estimate=pl.CostEstimate(
            flops=8 * count * partners * width,
            bytes_accessed=12 * count * width + 2 * partners * width,
            transcendentals=2 * count * partners,
        ),
    )(factors, own_ids, other_ids, mine, theirs, *others)


def local(image_features, text_features, image_weight, text_weight, log_scale, logit_bias):
    scale = jnp.exp(log_scale[0])
    bias = logit_bias[0]
    zl, y, c, zh, x = (lax.axis_index(axis) for axis in ("zl", "y", "c", "zh", "x"))
    rows, depth = image_features.shape
    width = image_weight.shape[1]
    own = rows // SIZES["x"]

    with jax.named_scope("embed"):
        parts = [
            dot(features, weight, ((1,), (0,))).astype(BF16).reshape(SIZES["x"], own, width)
            for features, weight in ((image_features, image_weight), (text_features, text_weight))
        ]
        parts = exchange(jnp.concatenate(parts, axis=1), "x")
        embed = jnp.sum(parts.astype(F32), axis=0)
        embed = embed + shifted(embed, "zh", 1)
        inverse = lax.rsqrt(jnp.sum(embed * embed, axis=-1, keepdims=True) + EPS)
        unit = embed * inverse
        vec = unit.astype(BF16)
        kinds = vec.reshape(2, own, width)

    with jax.named_scope("gather_own"):
        own_vec = lax.dynamic_index_in_dim(kinds, zh, 0, keepdims=False)
        mine = spread(own_vec, "y", SIZES["y"]).reshape(-1, width)
        theirs = shifted(mine, "c", 1)

    with jax.named_scope("gather_others"):
        pair = jnp.stack([kinds, along_z(vec, 4).reshape(2, own, width)], axis=1)
        pair = pair.reshape(2, 2 * own, width)
        at = zh * SIZES["zl"] + zl
        column = []
        for by in (0, 1, -1, 2):
            half = (at + by + 2 * SIZES["zl"]) // SIZES["zl"] % 2
            block = jnp.where(half == 0, pair[1], pair[0])
            column.append(along_z(block, by) if by else block)
        column = jnp.concatenate(column)
        others = [column] + [shifted(column, "x", by) for by in STEPS[1:]]

    with jax.named_scope("pairs"):
        hc, hy, hrow = flat(2, SIZES["y"], own)
        held_data = (zl * SIZES["y"] + hy) * 2 + jnp.where(hc == 0, c, 1 - c)
        held_id = held_data * rows + x * own + hrow
        orow = lax.iota(jnp.int32, own)
        other_id = []
        for step in STEPS:
            for group in GROUPS:
                data = ((zl + group + SIZES["zl"]) % SIZES["zl"] * SIZES["y"] + y) * 2 + c
                place = (x - step + SIZES["x"]) % SIZES["x"]
                other_id.append(data * rows + place * own + orow)
        mine_sum, theirs_sum = pair_sums(
            jnp.stack([scale, bias]),
            held_id[:, None],
            jnp.concatenate(other_id)[None, :],
            mine,
            theirs,
            others,
        )

    with jax.named_scope("reduce_pairs"):
        direction = mine_sum + shifted(theirs_sum, "c", 1)
        direction = exchange(direction.astype(BF16).reshape(SIZES["y"], own, width), "y")
        direction = scale * jnp.sum(direction.astype(F32), axis=0)

    with jax.named_scope("back"):
        unit = lax.dynamic_index_in_dim(unit.reshape(2, own, width), zh, 0, keepdims=False)
        inverse = lax.dynamic_index_in_dim(inverse.reshape(2, own, 1), zh, 0, keepdims=False)
        inner = jnp.sum(unit * direction, axis=-1, keepdims=True)
        back = (inverse * (direction - unit * inner)).astype(BF16)
        swapped = shifted(back, "zh", 1)
        back = jnp.concatenate(
            [jnp.where(zh == 0, back, swapped), jnp.where(zh == 0, swapped, back)]
        )
        back = spread(back, "x", SIZES["x"]).reshape(-1, width)

    with jax.named_scope("feature_grad"):
        weights = jnp.concatenate([image_weight, text_weight])
        grads = dot(back, weights, ((1,), (1,))).reshape(SIZES["x"], 2, own, 2 * depth)
        image_feature_grad = grads[:, 0, :, :depth].reshape(rows, depth)
        text_feature_grad = grads[:, 1, :, depth:].reshape(rows, depth)

    with jax.named_scope("weight_grad"):
        blank = jnp.zeros((SIZES["x"], own, depth), BF16)
        features = jnp.concatenate(
            [
                jnp.concatenate([image_features.reshape(SIZES["x"], own, depth), blank], axis=2),
                jnp.concatenate([blank, text_features.reshape(SIZES["x"], own, depth)], axis=2),
            ],
            axis=1,
        ).reshape(2 * rows, 2 * depth)
        chips = SIZES["zl"] * SIZES["y"]
        share = width // (chips * 2)
        pc, pchip, pk = flat(2, chips, share)
        source = (pchip * 2 + jnp.where(pc == 0, c, 1 - c)) * share + pk
        order = lax.broadcasted_iota(jnp.int32, (width, width), 0) == source[None, :]
        sorted_back = dot(back, order.astype(BF16), ((1,), (0,))).astype(BF16)
        partial = dot(sorted_back, features, ((0,), (0,)))
        partial = partial[: width // 2] + shifted(partial[width // 2 :], "c", 1)
        partial = exchange(partial.astype(BF16).reshape(chips, share, 2 * depth), ("zl", "y"))
        total = jnp.sum(partial.astype(F32), axis=0).T

    return (total[:depth], total[depth:], image_feature_grad, text_feature_grad)


def solution(mesh):
    names = ("zl", "y", "c", "zh", "x")
    fine = Mesh(mesh.devices.reshape([SIZES[name] for name in names]), names)
    placed = (P(DATA, TENSOR), P(DATA, TENSOR), P(TENSOR, None), P(TENSOR, None), P(), P())
    return jax.shard_map(
        local,
        mesh=fine,
        in_specs=placed,
        out_specs=(P(TENSOR, DATA), P(TENSOR, DATA), P(DATA, TENSOR), P(DATA, TENSOR)),
        check_vma=False,
    )
```

```python
import jax
import jax.numpy as jnp
from jax import lax
from jax.experimental import pallas as pl
from jax.experimental.pallas import tpu as pltpu
from jax.sharding import Mesh, PartitionSpec as P

EPS = 1e-06
DATA = ("zl", "y", "c")
TENSOR = ("zh", "x")
SIZES = {"zl": 8, "y": 8, "c": 2, "zh": 2, "x": 4}
STEPS = (0, 1, 3, 2)
GROUPS = (0, -4, -1, -5, 1, -3, -2, -6)
F32 = jnp.float32
BF16 = jnp.bfloat16


def dot(a, b, dims):
    return lax.dot_general(a, b, (dims, ((), ())), preferred_element_type=F32)


def exchange(blocks, axes):
    return lax.all_to_all(blocks, axes, 0, 0, tiled=True)


def spread(block, axes, count):
    return exchange(jnp.broadcast_to(block[None], (count, *block.shape)), axes)


def shifted(value, axis, by):
    size = SIZES[axis]
    return lax.ppermute(value, axis, [(i, (i + by) % size) for i in range(size)])


def along_z(value, by):
    size = SIZES["zh"] * SIZES["zl"]
    place = [(z % SIZES["zl"]) * SIZES["zh"] + z // SIZES["zl"] for z in range(size)]
    pairs = [(place[z], place[(z + by) % size]) for z in range(size)]
    return lax.ppermute(value, ("zl", "zh"), pairs)


def flat(*sizes):
    return [lax.broadcasted_iota(jnp.int32, sizes, i).reshape(-1) for i in range(len(sizes))]


def pair_kernel(factors, own_ids, other_ids, mine, theirs, *refs):
    blocks, (mine_sum, theirs_sum, held, partners) = refs[: len(STEPS)], refs[len(STEPS) :]
    for target, sources in ((held, (mine, theirs)), (partners, blocks)):
        size = sources[0].shape[0]
        for i, source in enumerate(sources):
            target[i * size : (i + 1) * size, :] = source[...]
    other = partners[...]
    logits = factors[0] * dot(held[...], other, ((1,), (1,))) + factors[1]
    coef = jax.nn.sigmoid(logits) - jnp.where(own_ids[...] == other_ids[...], 1.0, 0.0)
    total = dot(coef.astype(BF16), other, ((1,), (0,)))
    count = mine.shape[0]
    mine_sum[...] = total[:count]
    theirs_sum[...] = total[count:]


def pair_sums(factors, own_ids, other_ids, mine, theirs, others):
    count, width = mine.shape
    partners = len(others) * others[0].shape[0]
    whole = pl.BlockSpec(memory_space=pltpu.VMEM)
    out = jax.ShapeDtypeStruct((count, width), F32)
    return pl.pallas_call(
        pair_kernel,
        out_shape=(out, out),
        in_specs=[pl.BlockSpec(memory_space=pltpu.SMEM)] + [whole] * (4 + len(others)),
        out_specs=(whole, whole),
        scratch_shapes=[pltpu.VMEM((2 * count, width), BF16), pltpu.VMEM((partners, width), BF16)],
        compiler_params=pltpu.CompilerParams(vmem_limit_bytes=24 * 2**20),
        cost_estimate=pl.CostEstimate(
            flops=8 * count * partners * width,
            bytes_accessed=12 * count * width + 2 * partners * width,
            transcendentals=2 * count * partners,
        ),
    )(factors, own_ids, other_ids, mine, theirs, *others)


def local(image_features, text_features, image_weight, text_weight, log_scale, logit_bias):
    scale = jnp.exp(log_scale[0])
    bias = logit_bias[0]
    zl, y, c, zh, x = (lax.axis_index(axis) for axis in ("zl", "y", "c", "zh", "x"))
    rows, depth = image_features.shape
    width = image_weight.shape[1]
    own = rows // SIZES["x"]

    with jax.named_scope("embed"):
        parts = [
            dot(features, weight, ((1,), (0,))).astype(BF16).reshape(SIZES["x"], own, width)
            for features, weight in ((image_features, image_weight), (text_features, text_weight))
        ]
        parts = exchange(jnp.concatenate(parts, axis=1), "x")
        embed = jnp.sum(parts.astype(F32), axis=0)
        other_half, below, above = along_z(embed, 8), along_z(embed, 4), along_z(embed, -4)
        embeds = jnp.concatenate([embed + other_half, below + above])
        inverse = lax.rsqrt(jnp.sum(embeds * embeds, axis=-1, keepdims=True) + EPS)
        unit = embeds * inverse
        pair = unit.astype(BF16).reshape(2, 2, own, width)
        unit, inverse, kinds = unit[: 2 * own], inverse[: 2 * own], pair[0]

    with jax.named_scope("gather_own"):
        own_vec = lax.dynamic_index_in_dim(kinds, zh, 0, keepdims=False)
        mine = spread(own_vec, "y", SIZES["y"]).reshape(-1, width)
        theirs = shifted(mine, "c", 1)

    with jax.named_scope("gather_others"):
        pair = pair.transpose(1, 0, 2, 3).reshape(2, 2 * own, width)
        at = zh * SIZES["zl"] + zl
        column = []
        for by in (0, 1, -1, 2):
            half = (at + by + 2 * SIZES["zl"]) // SIZES["zl"] % 2
            block = jnp.where(half == 0, pair[1], pair[0])
            column.append(along_z(block, by) if by else block)
        column = jnp.concatenate(column)
        others = [column] + [shifted(column, "x", by) for by in STEPS[1:]]

    with jax.named_scope("pairs"):
        hc, hy, hrow = flat(2, SIZES["y"], own)
        held_data = (zl * SIZES["y"] + hy) * 2 + jnp.where(hc == 0, c, 1 - c)
        held_id = held_data * rows + x * own + hrow
        orow = lax.iota(jnp.int32, own)
        other_id = []
        for step in STEPS:
            for group in GROUPS:
                data = ((zl + group + SIZES["zl"]) % SIZES["zl"] * SIZES["y"] + y) * 2 + c
                place = (x - step + SIZES["x"]) % SIZES["x"]
                other_id.append(data * rows + place * own + orow)
        mine_sum, theirs_sum = pair_sums(
            jnp.stack([scale, bias]),
            held_id[:, None],
            jnp.concatenate(other_id)[None, :],
            mine,
            theirs,
            others,
        )

    with jax.named_scope("reduce_pairs"):
        direction = mine_sum + shifted(theirs_sum, "c", 1)
        direction = exchange(direction.astype(BF16).reshape(SIZES["y"], own, width), "y")
        direction = scale * jnp.sum(direction.astype(F32), axis=0)

    with jax.named_scope("back"):
        unit = lax.dynamic_index_in_dim(unit.reshape(2, own, width), zh, 0, keepdims=False)
        inverse = lax.dynamic_index_in_dim(inverse.reshape(2, own, 1), zh, 0, keepdims=False)
        inner = jnp.sum(unit * direction, axis=-1, keepdims=True)
        back = (inverse * (direction - unit * inner)).astype(BF16)
        swapped = shifted(back, "zh", 1)
        back = jnp.concatenate(
            [jnp.where(zh == 0, back, swapped), jnp.where(zh == 0, swapped, back)]
        )
        back = spread(back, "x", SIZES["x"]).reshape(-1, width)

    with jax.named_scope("feature_grad"):
        weights = jnp.concatenate([image_weight, text_weight])
        grads = dot(back, weights, ((1,), (1,))).reshape(SIZES["x"], 2, own, 2 * depth)
        image_feature_grad = grads[:, 0, :, :depth].reshape(rows, depth)
        text_feature_grad = grads[:, 1, :, depth:].reshape(rows, depth)

    with jax.named_scope("weight_grad"):
        blank = jnp.zeros((SIZES["x"], own, depth), BF16)
        features = jnp.concatenate(
            [
                jnp.concatenate([image_features.reshape(SIZES["x"], own, depth), blank], axis=2),
                jnp.concatenate([blank, text_features.reshape(SIZES["x"], own, depth)], axis=2),
            ],
            axis=1,
        ).reshape(2 * rows, 2 * depth)
        chips = SIZES["zl"] * SIZES["y"]
        share = width // (chips * 2)
        pc, pchip, pk = flat(2, chips, share)
        source = (pchip * 2 + jnp.where(pc == 0, c, 1 - c)) * share + pk
        order = lax.broadcasted_iota(jnp.int32, (width, width), 0) == source[None, :]
        sorted_back = dot(back, order.astype(BF16), ((1,), (0,))).astype(BF16)
        partial = dot(sorted_back, features, ((0,), (0,)))
        partial = partial[: width // 2] + shifted(partial[width // 2 :], "c", 1)
        partial = exchange(partial.astype(BF16).reshape(chips, share, 2 * depth), ("zl", "y"))
        total = jnp.sum(partial.astype(F32), axis=0).T

    return (total[:depth], total[depth:], image_feature_grad, text_feature_grad)


def solution(mesh):
    names = ("zl", "y", "c", "zh", "x")
    fine = Mesh(mesh.devices.reshape([SIZES[name] for name in names]), names)
    placed = (P(DATA, TENSOR), P(DATA, TENSOR), P(TENSOR, None), P(TENSOR, None), P(), P())
    return jax.shard_map(
        local,
        mesh=fine,
        in_specs=placed,
        out_specs=(P(TENSOR, DATA), P(TENSOR, DATA), P(DATA, TENSOR), P(DATA, TENSOR)),
        check_vma=False,
    )
```

```python
import jax
import jax.numpy as jnp
from jax import lax
from jax.experimental import pallas as pl
from jax.experimental.pallas import tpu as pltpu
from jax.sharding import Mesh, PartitionSpec as P

EPS = 1e-06
DATA = ("zl", "y", "c")
TENSOR = ("zh", "x")
SIZES = {"zl": 8, "y": 8, "c": 2, "zh": 2, "x": 4}
STEPS = (0, 1, 3, 2)
GROUPS = (0, -4, -1, -5, 1, -3, -2, -6)
F32 = jnp.float32
BF16 = jnp.bfloat16


def dot(a, b, dims):
    return lax.dot_general(a, b, (dims, ((), ())), preferred_element_type=F32)


def exchange(blocks, axes):
    return lax.all_to_all(blocks, axes, 0, 0, tiled=True)


def spread(block, axes, count):
    return exchange(jnp.broadcast_to(block[None], (count, *block.shape)), axes)


def shifted(value, axis, by):
    size = SIZES[axis]
    return lax.ppermute(value, axis, [(i, (i + by) % size) for i in range(size)])


def along_z(value, by):
    size = SIZES["zh"] * SIZES["zl"]
    place = [(z % SIZES["zl"]) * SIZES["zh"] + z // SIZES["zl"] for z in range(size)]
    pairs = [(place[z], place[(z + by) % size]) for z in range(size)]
    return lax.ppermute(value, ("zl", "zh"), pairs)


def flat(*sizes):
    return [lax.broadcasted_iota(jnp.int32, sizes, i).reshape(-1) for i in range(len(sizes))]


def pair_kernel(factors, own_ids, other_ids, mine, theirs, *refs):
    blocks, (mine_sum, theirs_sum, held, partners) = refs[: len(STEPS)], refs[len(STEPS) :]
    for target, sources in ((held, (mine, theirs)), (partners, blocks)):
        size = sources[0].shape[0]
        for i, source in enumerate(sources):
            target[i * size : (i + 1) * size, :] = source[...]
    other = partners[...]
    logits = factors[0] * dot(held[...], other, ((1,), (1,))) + factors[1]
    coef = jax.nn.sigmoid(logits) - jnp.where(own_ids[...] == other_ids[...], 1.0, 0.0)
    total = dot(coef.astype(BF16), other, ((1,), (0,)))
    count = mine.shape[0]
    mine_sum[...] = total[:count]
    theirs_sum[...] = total[count:]


def pair_sums(factors, own_ids, other_ids, mine, theirs, others):
    count, width = mine.shape
    partners = len(others) * others[0].shape[0]
    whole = pl.BlockSpec(memory_space=pltpu.VMEM)
    out = jax.ShapeDtypeStruct((count, width), F32)
    return pl.pallas_call(
        pair_kernel,
        out_shape=(out, out),
        in_specs=[pl.BlockSpec(memory_space=pltpu.SMEM)] + [whole] * (4 + len(others)),
        out_specs=(whole, whole),
        scratch_shapes=[pltpu.VMEM((2 * count, width), BF16), pltpu.VMEM((partners, width), BF16)],
        compiler_params=pltpu.CompilerParams(vmem_limit_bytes=24 * 2**20),
        cost_estimate=pl.CostEstimate(
            flops=8 * count * partners * width,
            bytes_accessed=12 * count * width + 2 * partners * width,
            transcendentals=2 * count * partners,
        ),
    )(factors, own_ids, other_ids, mine, theirs, *others)


def local(image_features, text_features, image_weight, text_weight, log_scale, logit_bias):
    scale = jnp.exp(log_scale[0])
    bias = logit_bias[0]
    zl, y, c, zh, x = (lax.axis_index(axis) for axis in ("zl", "y", "c", "zh", "x"))
    rows, depth = image_features.shape
    width = image_weight.shape[1]
    own = rows // SIZES["x"]

    with jax.named_scope("embed"):
        parts = [
            dot(features, weight, ((1,), (0,))).astype(BF16).reshape(SIZES["x"], own, width)
            for features, weight in ((image_features, image_weight), (text_features, text_weight))
        ]
        parts = exchange(jnp.concatenate(parts, axis=1), "x")
        embed = jnp.sum(parts.astype(F32), axis=0)
        embed = embed + shifted(embed, "zh", 1)
        inverse = lax.rsqrt(jnp.sum(embed * embed, axis=-1, keepdims=True) + EPS)
        unit = embed * inverse
        vec = unit.astype(BF16)
        kinds = vec.reshape(2, own, width)

    with jax.named_scope("gather_own"):
        own_vec = lax.dynamic_index_in_dim(kinds, zh, 0, keepdims=False)
        mine = spread(own_vec, "y", SIZES["y"]).reshape(-1, width)
        theirs = shifted(mine, "c", 1)

    with jax.named_scope("gather_others"):
        pair = jnp.stack([kinds, along_z(vec, 4).reshape(2, own, width)], axis=1)
        pair = pair.reshape(2, 2 * own, width)
        at = zh * SIZES["zl"] + zl
        column = []
        for by in (0, 1, -1, 2):
            half = (at + by + 2 * SIZES["zl"]) // SIZES["zl"] % 2
            block = jnp.where(half == 0, pair[1], pair[0])
            column.append(along_z(block, by) if by else block)
        column = jnp.concatenate(column)
        others = [column] + [shifted(column, "x", by) for by in STEPS[1:]]

    with jax.named_scope("pairs"):
        hc, hy, hrow = flat(2, SIZES["y"], own)
        held_data = (zl * SIZES["y"] + hy) * 2 + jnp.where(hc == 0, c, 1 - c)
        held_id = held_data * rows + x * own + hrow
        orow = lax.iota(jnp.int32, own)
        other_id = []
        for step in STEPS:
            for group in GROUPS:
                data = ((zl + group + SIZES["zl"]) % SIZES["zl"] * SIZES["y"] + y) * 2 + c
                place = (x - step + SIZES["x"]) % SIZES["x"]
                other_id.append(data * rows + place * own + orow)
        mine_sum, theirs_sum = pair_sums(
            jnp.stack([scale, bias]),
            held_id[:, None],
            jnp.concatenate(other_id)[None, :],
            mine,
            theirs,
            others,
        )

    with jax.named_scope("reduce_pairs"):
        direction = mine_sum + shifted(theirs_sum, "c", 1)
        direction = exchange(direction.astype(BF16).reshape(SIZES["y"], own, width), "y")
        direction = scale * jnp.sum(direction.astype(F32), axis=0)

    with jax.named_scope("back"):
        unit = lax.dynamic_index_in_dim(unit.reshape(2, own, width), zh, 0, keepdims=False)
        inverse = lax.dynamic_index_in_dim(inverse.reshape(2, own, 1), zh, 0, keepdims=False)
        inner = jnp.sum(unit * direction, axis=-1, keepdims=True)
        back = (inverse * (direction - unit * inner)).astype(BF16)
        back = spread(back, "x", SIZES["x"]).reshape(-1, width)
        swapped = shifted(back, "zh", 1)

    with jax.named_scope("feature_grad"):
        weights = jnp.concatenate([image_weight, text_weight])
        own_grads = dot(back, weights, ((1,), (1,)))
        other_grads = dot(swapped, weights, ((1,), (1,)))
        image_feature_grad = jnp.where(zh == 0, own_grads[:, :depth], other_grads[:, :depth])
        text_feature_grad = jnp.where(zh == 0, other_grads[:, depth:], own_grads[:, depth:])

    with jax.named_scope("weight_grad"):
        blank = jnp.zeros((rows, depth), BF16)
        image_block = jnp.concatenate([image_features, blank], axis=1)
        text_block = jnp.concatenate([blank, text_features], axis=1)
        own_block = jnp.where(zh == 0, image_block, text_block)
        other_block = jnp.where(zh == 0, text_block, image_block)
        chips = SIZES["zl"] * SIZES["y"]
        share = width // (chips * 2)
        pc, pchip, pk = flat(2, chips, share)
        source = (pchip * 2 + jnp.where(pc == 0, c, 1 - c)) * share + pk
        order = lax.broadcasted_iota(jnp.int32, (width, width), 0) == source[None, :]
        order = order.astype(BF16)
        partial = 0.0
        for rows_back, block in ((back, own_block), (swapped, other_block)):
            sorted_back = dot(rows_back, order, ((1,), (0,))).astype(BF16)
            partial = partial + dot(sorted_back, block, ((0,), (0,)))
        partial = partial[: width // 2] + shifted(partial[width // 2 :], "c", 1)
        partial = exchange(partial.astype(BF16).reshape(chips, share, 2 * depth), ("zl", "y"))
        total = jnp.sum(partial.astype(F32), axis=0).T

    return (total[:depth], total[depth:], image_feature_grad, text_feature_grad)


def solution(mesh):
    names = ("zl", "y", "c", "zh", "x")
    fine = Mesh(mesh.devices.reshape([SIZES[name] for name in names]), names)
    placed = (P(DATA, TENSOR), P(DATA, TENSOR), P(TENSOR, None), P(TENSOR, None), P(), P())
    return jax.shard_map(
        local,
        mesh=fine,
        in_specs=placed,
        out_specs=(P(TENSOR, DATA), P(TENSOR, DATA), P(DATA, TENSOR), P(DATA, TENSOR)),
        check_vma=False,
    )
```
